32 devices in a mesh: req: 8 (over z, x), tp: 4 (over y, core).
Axes of the slice: x: 2, y: 2, z: 4, core: 2. Of those that a mesh axis runs over, the one named last changes fastest.
Arguments:
- queries: bfloat16 [1024, 3584], P('req', 'tp'), may hold values from -13 to 13
- tree_kv: bfloat16 [1024, 4, 256], P('req', 'tp'), may hold values from -5 to 5
- page_pool: bfloat16 [96, 4, 128, 256], P('req', 'tp'), may hold values from -5 to 5
- page_table: int32 [16, 8], P('req'), may hold values from 0 to 11, as said below
- cache_len: int32 [16], P('req'), may hold values from 1 to 1024
- parents: int32 [16, 64], P('req'), may hold values from -1 to 62, as said below
- accepted: int32 [16], P('req'), may hold values from 0 to 63
- o_weight: bfloat16 [3584, 1792], P('tp'), may hold values from -0.5 to 0.5
Outputs:
- projected: bfloat16 [1024, 1792], P(('req', 'tp'))
- kept_rows: bfloat16 [1024, 4, 256], P('req', 'tp')
The draws below stay inside these ranges and needn't reach their ends.
Inputs may be any that keep to these rules, and one draw needn't show every extreme that they name: Logical page k of request r is in slot page_table[r, k] of its own device's pool for k < 2, among that pool's first 4 slots, and for k >= 2 in that slot of the next req device's pool (the first device after the last), among its last 8 slots; distinct pages are in distinct slots; entries at k >= ceil(cache_len[r] / 128) are 0. parents[r, 0] = -1 and 0 <= parents[r, j] < j for j >= 1.
All inputs are finite; a program needn't handle non-finite values.
Results may differ from the reference program's by a relative error of at most 0.007.
Values may be sent and summed in bfloat16 or wider, within the bound.
A program may use at most 64 MiB of HBM per device.

```python
import math
import jax
import jax.numpy as jnp
from jax import lax

HQ = 28
KVH = 4
HEAD_SIZE = 128
D_WIN = 1792
PAGE = 128
TREE = 64
MAXP = 8
LOCAL = 2
SPILL_PAGES = 8
REQ_DEV = 2
REQS = 16
TOKENS = 1024
POOL = 12
PAGES_ALL = 96
N_REQ = 8


def page_layout(key):
    devices = REQS // REQ_DEV
    own_slots = REQ_DEV * LOCAL
    request_ids = jnp.arange(REQ_DEV, dtype=jnp.int32)[None, :]
    device_ids = jnp.arange(devices, dtype=jnp.int32)[:, None]
    big_request = jax.random.randint(jax.random.fold_in(key, 11), (devices, 1), 0, REQ_DEV)
    big_pages = jax.random.randint(jax.random.fold_in(key, 12), (devices, 1), LOCAL + 1, MAXP + 1)
    big_pages = jnp.where(device_ids == 0, MAXP, big_pages)
    room = SPILL_PAGES - (big_pages - LOCAL)
    other_offset = jax.random.randint(jax.random.fold_in(key, 13), (devices, 1), 1, max(REQ_DEV, 2))
    second = (big_request + other_offset) % REQ_DEV
    extra = jax.random.randint(jax.random.fold_in(key, 14), (devices, 1), 0, room + 1)
    extra = jnp.minimum(extra, MAXP - LOCAL)
    small_pages = jax.random.randint(jax.random.fold_in(key, 15), (devices, REQ_DEV), 1, LOCAL + 1)
    is_second = (request_ids == second) & (second != big_request) & (extra > 0)
    pages = jnp.where(request_ids == big_request, big_pages, jnp.where(is_second, LOCAL + extra, small_pages))
    last_fill = jax.random.randint(jax.random.fold_in(key, 16), (devices, REQ_DEV), 1, PAGE + 1)
    lengths = (pages - 1) * PAGE + last_fill
    lengths = jnp.where((device_ids == 0) & (request_ids == big_request), MAXP * PAGE, lengths)
    spilled = jnp.maximum(pages - LOCAL, 0)
    before = jnp.cumsum(spilled, axis=1) - spilled
    own_perm = jax.vmap(lambda sub: jax.random.permutation(sub, own_slots))(jax.random.split(jax.random.fold_in(key, 17), devices))
    spill_perm = jax.vmap(lambda sub: jax.random.permutation(sub, SPILL_PAGES))(jax.random.split(jax.random.fold_in(key, 18), devices))
    page_ids = jnp.arange(MAXP, dtype=jnp.int32)[None, None, :]
    own_pos = request_ids[:, :, None] * LOCAL + jnp.minimum(page_ids, LOCAL - 1)
    own_pos = jnp.broadcast_to(own_pos, (devices, REQ_DEV, MAXP)).reshape(devices, REQ_DEV * MAXP)
    own_slot = jnp.take_along_axis(own_perm, own_pos, axis=1).reshape(devices, REQ_DEV, MAXP)
    spill_pos = jnp.clip(before[:, :, None] + page_ids - LOCAL, 0, SPILL_PAGES - 1).reshape(devices, REQ_DEV * MAXP)
    spill_slot = own_slots + jnp.take_along_axis(spill_perm, spill_pos, axis=1).reshape(devices, REQ_DEV, MAXP)
    table = jnp.where(page_ids < LOCAL, own_slot, spill_slot)
    table = jnp.where(page_ids < pages[:, :, None], table, 0)
    return (table.reshape(REQS, MAXP).astype(jnp.int32), lengths.reshape(REQS).astype(jnp.int32))


def draw_page_table(key, part):
    return page_layout(key)[0]


def draw_cache_len(key, part):
    return page_layout(key)[1]


def draw_parents(key, part):
    node_ids = jnp.arange(TREE, dtype=jnp.int32)[None, :]
    back_steps = jax.random.randint(key, (REQS, TREE), 0, 8)
    parent_ids = jnp.maximum(node_ids - 1 - back_steps, 0)
    return jnp.where(node_ids == 0, -1, parent_ids).astype(jnp.int32)


def key_value_block(key, shape):
    block = jax.random.normal(key, shape, jnp.float32)
    return jnp.clip(block, -5.0, 5.0).astype(jnp.bfloat16)


def draw_tree_kv(key, part):
    return key_value_block(key, (TOKENS, KVH, 2 * HEAD_SIZE))


def draw_page_pool(key, part):
    return key_value_block(key, (PAGES_ALL, KVH, PAGE, 2 * HEAD_SIZE))


def draw_queries(key, part):
    shape = (TOKENS, HQ * HEAD_SIZE)
    block = jax.random.normal(key, shape, jnp.float32)
    return jnp.clip(block, -13.0, 13.0).astype(jnp.bfloat16)


def with_ends(values, own_key, smallest, largest):
    longest = values.shape.index(max(values.shape))
    spots = []
    for shift in (0, 1):
        where = [jax.random.randint(jax.random.fold_in(own_key, axis), (), 0, length) for axis, length in enumerate(values.shape)]
        where[longest] = (where[longest] + shift) % values.shape[longest]
        spots.append(tuple(where))
    return values.at[spots[0]].set(smallest).at[spots[1]].set(largest)


def block_levels(rng, extent, cuts, low, top_value):
    loudness, own = 1.0, jax.random.fold_in(rng, 6)
    for axis_at, shards_of in cuts:
        steps = jnp.exp(jax.random.uniform(jax.random.fold_in(own, axis_at), (shards_of,), jnp.float32, low / len(cuts), top_value / len(cuts)))
        loudness = loudness * jnp.repeat(steps, extent[axis_at] // shards_of).reshape([-1 if axis == axis_at else 1 for axis in range(len(extent))])
    return loudness


def bell_draw(stream_key, shape, deviation, most, pieces=(), held_as=jnp.bfloat16):
    drawn = deviation * jax.random.normal(stream_key, shape, jnp.float32)
    if pieces:
        drawn = drawn * block_levels(stream_key, shape, pieces, -0.22, 0.18)
    return jnp.clip(drawn, -most, most).astype(held_as)


def setup_inputs(seed: int = 0) -> dict:
    key_of = jax.random.split(jax.random.key(seed), 9)
    return {
        "queries": draw_queries(jax.random.fold_in(key_of[8], 71), 0),
        "tree_kv": draw_tree_kv(jax.random.fold_in(key_of[8], 71), 0),
        "page_pool": draw_page_pool(jax.random.fold_in(key_of[8], 71), 0),
        "page_table": draw_page_table(jax.random.fold_in(key_of[8], 71), 0),
        "cache_len": draw_cache_len(jax.random.fold_in(key_of[8], 71), 0),
        "parents": draw_parents(jax.random.fold_in(key_of[8], 71), 0),
        "accepted": with_ends(jax.random.randint(key_of[6], (REQS,), 0, TREE), jax.random.fold_in(key_of[6], 1), 0, TREE - 1).astype(jnp.int32),
        "o_weight": bell_draw(key_of[7], (HQ * HEAD_SIZE, D_WIN), HEAD_SIZE ** -0.5, 0.5, ((0, 4),)),
    }


very_negative = -1e+30

def ancestors(parent_row):
    tree_len = parent_row.shape[0]
    node_ids = jnp.arange(tree_len, dtype=jnp.int32)
    parent_links = (parent_row[:, None] == node_ids[None, :]).astype(jnp.float32)
    reachable = jnp.eye(tree_len, dtype=jnp.float32) + parent_links
    for squaring in range((tree_len - 1).bit_length()):
        reachable = jnp.minimum(jnp.dot(reachable, reachable, precision=lax.Precision.HIGHEST), 1.0)
    return reachable

def reference(queries, tree_kv, page_pool, page_table, cache_len, parents, accepted, o_weight):
    group_size = HQ // KVH
    logit_scale = 1.0 / math.sqrt(HEAD_SIZE)
    query_rows = queries.reshape(REQS, TREE, KVH, group_size, HEAD_SIZE)
    tree_rows = tree_kv.reshape(REQS, TREE, KVH, 2 * HEAD_SIZE)
    home_device = jnp.arange(REQS, dtype=jnp.int32) // REQ_DEV
    page_ids = jnp.arange(MAXP, dtype=jnp.int32)
    offsets = jnp.arange(PAGE, dtype=jnp.int32)

    def one_request(request_data):
        request_query, request_draft_tree, parent_row, length, table_row, home, leaf_node = request_data
        owner_device = jnp.where(page_ids < LOCAL, home, (home + 1) % N_REQ)
        global_page = (owner_device * POOL + table_row).astype(jnp.int32)
        pages = page_pool[global_page]
        npages = (length + PAGE - 1) // PAGE
        visible = (page_ids[:, None] * PAGE + offsets[None, :] < length) & (page_ids[:, None] < npages)
        query_widened = request_query.astype(jnp.float32)
        scores = jnp.einsum('thgd,khnd->htgkn', query_widened, pages[..., :HEAD_SIZE].astype(jnp.float32)) * logit_scale
        page_mask = visible[None, None, None, :, :]
        scores = jnp.where(page_mask, scores, very_negative)
        maxima = lax.optimization_barrier(jnp.max(scores, axis=-1))
        weights = jnp.where(page_mask, jnp.exp(scores - maxima[..., None]), 0.0).astype(jnp.bfloat16)
        totals = lax.optimization_barrier(jnp.sum(weights.astype(jnp.float32), axis=-1))
        accums = jnp.einsum('htgkn,khnd->htgkd', weights.astype(jnp.float32), pages[..., HEAD_SIZE:].astype(jnp.float32))
        reachable = ancestors(parent_row)
        tree_mask = (reachable > 0.5)[None, :, None, :]
        tree_logits = jnp.einsum('qave,wae->aqvw', query_widened, request_draft_tree[..., :HEAD_SIZE].astype(jnp.float32)) * logit_scale
        tree_logits = jnp.where(tree_mask, tree_logits, very_negative)
        tree_max = lax.optimization_barrier(jnp.max(tree_logits, axis=-1))
        tree_probabilities = jnp.where(tree_mask, jnp.exp(tree_logits - tree_max[..., None]), 0.0).astype(jnp.bfloat16)
        tree_total = lax.optimization_barrier(jnp.sum(tree_probabilities.astype(jnp.float32), axis=-1))
        tree_running_sum = jnp.einsum('ieku,uiz->iekz', tree_probabilities.astype(jnp.float32), request_draft_tree[..., HEAD_SIZE:].astype(jnp.float32))
        overall = jnp.maximum(tree_max, lax.optimization_barrier(jnp.max(maxima, axis=-1)))
        page_factors = jnp.exp(maxima - overall[..., None])
        tree_factor = jnp.exp(tree_max - overall)
        numerator = lax.optimization_barrier(jnp.sum(page_factors[..., None] * accums, axis=3)) + tree_factor[..., None] * tree_running_sum
        denominator = lax.optimization_barrier(jnp.sum(page_factors * totals, axis=-1)) + tree_factor * tree_total
        normalized = (numerator / denominator[..., None]).astype(jnp.bfloat16)
        attention = jnp.transpose(normalized, (1, 0, 2, 3)).reshape(TREE, HQ * HEAD_SIZE)
        depths = lax.optimization_barrier(jnp.sum(reachable, axis=1)) - 1.0
        kept_mask = reachable[leaf_node]
        slot_ids = jnp.arange(TREE, dtype=jnp.float32)
        selector = kept_mask[None, :] * (depths[None, :] == slot_ids[:, None]).astype(jnp.float32)
        kept = jnp.einsum('sm,mhc->shc', selector, request_draft_tree.astype(jnp.float32)).astype(jnp.bfloat16)
        return (attention, kept)
    attention, kept = lax.map(one_request, (query_rows, tree_rows, parents, cache_len, page_table, home_device, accepted))
    projected = jnp.dot(attention.reshape(TOKENS, HQ * HEAD_SIZE), o_weight, preferred_element_type=jnp.float32).astype(jnp.bfloat16)
    return (projected, kept.reshape(TOKENS, KVH, 2 * HEAD_SIZE))
```

```python
import functools
import math

import jax
import jax.numpy as jnp
from jax import lax
from jax.experimental import pallas as pl
from jax.experimental.pallas import tpu as pltpu
from jax.sharding import PartitionSpec as P

HEAD_SIZE = 128
LOCAL = 2
COLS = 256
K_PIECES = 2
V_PIECES = 4

very_negative = -1e30
MESH = pl.DeviceIdType.MESH
f32 = jnp.float32
bf16 = jnp.bfloat16


def dot_t(a, b):
    return lax.dot_general(a, b, (((1,), (1,)), ((), ())), preferred_element_type=f32)


def kernel(
    table_ref,
    len_ref,
    acc_ref,
    parents_ref,
    q_hbm,
    tree_hbm,
    pool_hbm,
    w_hbm,
    out_ref,
    kept_ref,
    q_ref,
    tree_ref,
    own_ref,
    w_ref,
    k_ref,
    v_ref,
    s_ref,
    p_ref,
    sum_ref,
    att_ref,
    part_ref,
    send1,
    recv1,
    send2,
    recv2,
    load_sems,
    ks_sems,
    kr_sems,
    vs_sems,
    vr_sems,
    s1_sems,
    r1_sems,
    s2_sems,
    r2_sems,
):
    requests, max_pages = table_ref.shape
    tree = parents_ref.shape[1]
    tokens = requests * tree
    page = pool_hbm.shape[1]
    spill = k_ref.shape[0]
    own = own_ref.shape[0]
    group = q_ref.shape[1] // HEAD_SIZE
    rows = group * tree
    chunks = part_ref.shape[0]
    tp_size = part_ref.shape[1]
    scale = 1.0 / math.sqrt(HEAD_SIZE)

    n = lax.axis_size("req")
    me = lax.axis_index("req")
    before, after = lax.rem(me + n - 1, n), lax.rem(me + 1, n)
    tp = lax.axis_index("tp")
    low, high = lax.rem(tp, 2), tp // 2
    mate1 = high * 2 + (1 - low)
    mate2 = (1 - high) * 2 + low

    loads = [
        pltpu.make_async_copy(src, dst, load_sems.at[i])
        for i, (src, dst) in enumerate(
            (
                (q_hbm, q_ref),
                (tree_hbm, tree_ref),
                (pool_hbm.at[pl.ds(0, own)], own_ref),
                (w_hbm, w_ref),
            )
        )
    ]
    for load in loads:
        load.start()

    barrier = pltpu.get_barrier_semaphore()
    for where in ({"req": before}, {"req": after}, {"tp": mate1}, {"tp": mate2}):
        pl.semaphore_signal(barrier, inc=1, device_id=where, device_id_type=MESH)
    pl.semaphore_wait(barrier, 4)

    kn, vn = spill // K_PIECES, spill // V_PIECES
    k_copies = [
        pltpu.make_async_remote_copy(
            src_ref=pool_hbm.at[pl.ds(own + i * kn, kn), :, pl.ds(0, HEAD_SIZE)],
            dst_ref=k_ref.at[pl.ds(i * kn, kn)],
            send_sem=ks_sems.at[i],
            recv_sem=kr_sems.at[i],
            device_id={"req": before},
            device_id_type=MESH,
        )
        for i in range(K_PIECES)
    ]
    v_copies = [
        pltpu.make_async_remote_copy(
            src_ref=pool_hbm.at[pl.ds(own + i * vn, vn), :, pl.ds(HEAD_SIZE, HEAD_SIZE)],
            dst_ref=v_ref.at[pl.ds(i * vn, vn)],
            send_sem=vs_sems.at[i],
            recv_sem=vr_sems.at[i],
            device_id={"req": before},
            device_id_type=MESH,
        )
        for i in range(V_PIECES)
    ]
    for copy in k_copies + v_copies:
        copy.start()

    square = (tokens, tokens)
    sub = lax.broadcasted_iota(jnp.int32, square, 0).astype(f32)
    lane = lax.broadcasted_iota(jnp.int32, square, 1).astype(f32)
    spread_sub = lax.broadcasted_iota(jnp.int32, (tree, tokens), 0)
    spread_lane = lax.broadcasted_iota(jnp.int32, (tree, tokens), 1)
    parents = parents_ref[...].astype(f32)
    parent_row = jnp.zeros((1, tokens), f32)
    for r in range(requests):
        shifted = jnp.where(parents[r : r + 1] < 0, 256.0, parents[r : r + 1] + r * tree)
        spread = (spread_sub + r * tree == spread_lane).astype(f32)
        parent_row += jnp.dot(shifted, spread, preferred_element_type=f32)
    reach_t = ((parent_row == sub) | (sub == lane)).astype(f32)
    for _ in range((tree - 1).bit_length()):
        half = reach_t.astype(bf16)
        reach_t = jnp.minimum(jnp.dot(half, half, preferred_element_type=f32), 1.0)
    reach = reach_t.T
    lane_row = lax.broadcasted_iota(jnp.int32, (1, tokens), 1)
    leaf = jnp.zeros(square, jnp.bool_)
    first_slot = jnp.zeros((1, tokens), f32)
    for r in range(requests):
        leaf = leaf | (sub == (acc_ref[r] + r * tree).astype(f32))
        first_slot = jnp.where(lane_row >= r * tree, float(r * tree), first_slot)
    kept_mask = jnp.sum(jnp.where(leaf, reach, 0.0), axis=0, keepdims=True)
    depth = jnp.sum(reach_t, axis=0, keepdims=True) - 1.0 + first_slot
    selector = jnp.where((depth == sub) & (kept_mask > 0.5), 1.0, 0.0).astype(bf16)
    loads[1].wait()
    kept = jnp.dot(selector, tree_ref[...], preferred_element_type=f32)
    kept_ref[...] = kept.astype(bf16)
    tree_bias = jnp.where(reach > 0.5, 0.0, very_negative)

    loads[0].wait()
    loads[2].wait()
    page_lane = lax.broadcasted_iota(jnp.int32, (1, page), 1)

    def bias_of(visible):
        return jnp.where(page_lane < visible, 0.0, very_negative)

    def query(r):
        return jnp.concatenate(
            [
                q_ref[r * tree : (r + 1) * tree, g * HEAD_SIZE : (g + 1) * HEAD_SIZE]
                for g in range(group)
            ],
            axis=0,
        )

    first = tokens + LOCAL * page
    for r in range(requests):
        q = query(r)
        s = dot_t(q, tree_ref[:, :HEAD_SIZE]).reshape(group, tree, tokens)
        s = s + tree_bias[r * tree : (r + 1) * tree][None]
        s_ref[r, :, 0:tokens] = s.reshape(rows, tokens)
        for k in range(LOCAL):
            keys = own_ref[table_ref[r, k]][:, :HEAD_SIZE]
            at = tokens + k * page
            s_ref[r, :, at : at + page] = dot_t(q, keys) + bias_of(len_ref[r] - k * page)

    for i in range(K_PIECES):
        k_copies[i].wait_recv()
        for r in range(requests):
            keys = k_ref[i * kn : (i + 1) * kn].reshape(kn * page, HEAD_SIZE)
            s = dot_t(query(r), keys)
            for j in range(kn):
                slot = i * kn + j
                visible = jnp.int32(0)
                for k in range(LOCAL, max_pages):
                    here = table_ref[r, k] == own + slot
                    visible = jnp.maximum(
                        visible, jnp.where(here, len_ref[r] - k * page, 0)
                    )
                at = first + slot * page
                s_ref[r, :, at : at + page] = s[:, j * page : (j + 1) * page] + bias_of(visible)

    width = s_ref.shape[2]
    for r in range(requests):

        def weigh(g, _):
            at = pl.ds(pl.multiple_of(g * tree, tree), tree)
            s = s_ref[r, at, :]
            top = jnp.max(s, axis=1, keepdims=True)
            p_ref[r, at, :] = jnp.exp((s - top) * scale).astype(bf16)
            return 0

        lax.fori_loop(0, group, weigh, 0)

    ones = jnp.ones((page, HEAD_SIZE), bf16)

    def with_ones(values):
        return jnp.concatenate([values, ones], axis=1)

    for r in range(requests):
        values = [with_ones(tree_ref[:, HEAD_SIZE:])] + [
            with_ones(own_ref[table_ref[r, k]][:, HEAD_SIZE:]) for k in range(LOCAL)
        ]
        sum_ref[r] = jnp.dot(
            p_ref[r, :, 0:first], jnp.concatenate(values, axis=0), preferred_element_type=f32
        )
    for i in range(V_PIECES):
        v_copies[i].wait_recv()
        values = jnp.concatenate([with_ones(v_ref[i * vn + j]) for j in range(vn)], axis=0)
        at = first + i * vn * page
        for r in range(requests):
            more = jnp.dot(
                p_ref[r, :, at : at + vn * page], values, preferred_element_type=f32
            )
            if i < V_PIECES - 1:
                sum_ref[r] += more
            else:
                total = sum_ref[r] + more
                attention = (total[:, :HEAD_SIZE] / total[:, HEAD_SIZE:]).astype(bf16)
                for g in range(group):
                    att_ref[
                        r * tree : (r + 1) * tree, g * HEAD_SIZE : (g + 1) * HEAD_SIZE
                    ] = attention[g * tree : (g + 1) * tree]

    loads[3].wait()
    out_rows = tokens // tp_size

    def first_copy(j):
        return pltpu.make_async_remote_copy(
            src_ref=send1.at[j, 1 - low],
            dst_ref=recv1.at[j],
            send_sem=s1_sems.at[j],
            recv_sem=r1_sems.at[j],
            device_id={"tp": mate1},
            device_id_type=MESH,
        )

    def second_copy(j):
        return pltpu.make_async_remote_copy(
            src_ref=send2.at[j],
            dst_ref=recv2.at[j],
            send_sem=s2_sems.at[j],
            recv_sem=r2_sems.at[j],
            device_id={"tp": mate2},
            device_id_type=MESH,
        )

    def pass_on(j):
        first_copy(j).wait_recv()
        theirs = part_ref[j, mate2] + recv1[j, 1 - high].astype(f32)
        send2[j] = theirs.astype(bf16)
        second_copy(j).start()

    for j in range(chunks):
        part = jnp.dot(
            att_ref[...], w_ref[:, j * COLS : (j + 1) * COLS], preferred_element_type=f32
        )
        for i in range(tp_size):
            piece = part[i * out_rows : (i + 1) * out_rows]
            part_ref[j, i] = piece
            send1[j, i % 2, i // 2] = piece.astype(bf16)
        first_copy(j).start()
        if j >= 2:
            pass_on(j - 2)
    for j in range(chunks - 2, chunks):
        pass_on(j)
    for j in range(chunks):
        second_copy(j).wait_recv()
        mine = part_ref[j, tp] + recv1[j, high].astype(f32) + recv2[j].astype(f32)
        out_ref[:, j * COLS : (j + 1) * COLS] = mine.astype(bf16)
    for copy in k_copies + v_copies:
        copy.wait_send()
    for j in range(chunks):
        first_copy(j).wait_send()
        second_copy(j).wait_send()


def shards(queries, tree_kv, page_pool, page_table, cache_len, parents, accepted, o_weight):
    requests = page_table.shape[0]
    tree = parents.shape[1]
    tokens, features = queries.shape
    pool, _, page, kv = page_pool.shape
    own = requests * LOCAL
    spill = pool - own
    rows = features // HEAD_SIZE * tree
    width = tokens + (LOCAL + spill) * page
    d_out = o_weight.shape[1]
    tp = lax.axis_size("tp")
    out_rows = tokens // tp
    chunks = d_out // COLS
    smem = pl.BlockSpec(memory_space=pltpu.SMEM)
    vmem = pl.BlockSpec(memory_space=pltpu.VMEM)
    anywhere = pl.BlockSpec(memory_space=pl.ANY)
    dma = pltpu.SemaphoreType.DMA
    projected, kept = pl.pallas_call(
        kernel,
        out_shape=(
            jax.ShapeDtypeStruct((out_rows, d_out), bf16),
            jax.ShapeDtypeStruct((tokens, kv), bf16),
        ),
        in_specs=[smem, smem, smem, vmem, anywhere, anywhere, anywhere, anywhere],
        out_specs=(vmem, vmem),
        scratch_shapes=[
            pltpu.VMEM((tokens, features), bf16),
            pltpu.VMEM((tokens, kv), bf16),
            pltpu.VMEM((own, page, kv), bf16),
            pltpu.VMEM(o_weight.shape, bf16),
            pltpu.VMEM((spill, page, HEAD_SIZE), bf16),
            pltpu.VMEM((spill, page, HEAD_SIZE), bf16),
            pltpu.VMEM((requests, rows, width), f32),
            pltpu.VMEM((requests, rows, width), bf16),
            pltpu.VMEM((requests, rows, 2 * HEAD_SIZE), f32),
            pltpu.VMEM((tokens, features), bf16),
            pltpu.VMEM((chunks, tp, out_rows, COLS), f32),
            pltpu.VMEM((chunks, 2, tp // 2, out_rows, COLS), bf16),
            pltpu.VMEM((chunks, tp // 2, out_rows, COLS), bf16),
            pltpu.VMEM((chunks, out_rows, COLS), bf16),
            pltpu.VMEM((chunks, out_rows, COLS), bf16),
            dma((4,)),
            dma((K_PIECES,)),
            dma((K_PIECES,)),
            dma((V_PIECES,)),
            dma((V_PIECES,)),
            dma((chunks,)),
            dma((chunks,)),
            dma((chunks,)),
            dma((chunks,)),
        ],
        compiler_params=pltpu.CompilerParams(
            collective_id=0, has_side_effects=True, vmem_limit_bytes=40 * 2**20
        ),
    )(
        page_table,
        cache_len,
        accepted,
        parents,
        queries,
        tree_kv.reshape(tokens, kv),
        page_pool.reshape(pool, page, kv),
        o_weight,
    )
    return projected, kept.reshape(tokens, 1, kv)


def solution(mesh):
    in_specs = (
        P("req", "tp"),
        P("req", "tp", None),
        P("req", "tp", None, None),
        P("req", None),
        P("req"),
        P("req", None),
        P("req"),
        P("tp", None),
    )
    out_specs = (P(("req", "tp"), None), P("req", "tp", None))
    return jax.shard_map(shards, mesh=mesh, in_specs=in_specs, out_specs=out_specs, check_vma=False)
```

```python
import functools
import math

import jax
import jax.numpy as jnp
from jax import lax
from jax.experimental import pallas as pl
from jax.experimental.pallas import tpu as pltpu
from jax.sharding import PartitionSpec as P

HEAD_SIZE = 128
LOCAL = 2
COLS = 896
K_PIECES = 2
V_PIECES = 4

very_negative = -1e30
MESH = pl.DeviceIdType.MESH
f32 = jnp.float32
bf16 = jnp.bfloat16


def dot_t(a, b):
    return lax.dot_general(a, b, (((1,), (1,)), ((), ())), preferred_element_type=f32)


def kernel(
    table_ref,
    len_ref,
    acc_ref,
    parents_ref,
    q_hbm,
    tree_hbm,
    pool_hbm,
    w_hbm,
    out_ref,
    kept_ref,
    q_ref,
    tree_ref,
    own_ref,
    w_ref,
    k_ref,
    v_ref,
    s_ref,
    p_ref,
    sum_ref,
    att_ref,
    part_ref,
    send1,
    recv1,
    send2,
    recv2,
    load_sems,
    ks_sems,
    kr_sems,
    vs_sems,
    vr_sems,
    s1_sems,
    r1_sems,
    s2_sems,
    r2_sems,
):
    requests, max_pages = table_ref.shape
    tree = parents_ref.shape[1]
    tokens = requests * tree
    page = pool_hbm.shape[1]
    spill = k_ref.shape[0]
    own = own_ref.shape[0]
    group = q_ref.shape[1] // HEAD_SIZE
    rows = group * tree
    chunks = part_ref.shape[0]
    tp_size = part_ref.shape[1]
    scale = 1.0 / math.sqrt(HEAD_SIZE)

    n = lax.axis_size("req")
    me = lax.axis_index("req")
    before, after = lax.rem(me + n - 1, n), lax.rem(me + 1, n)
    tp = lax.axis_index("tp")
    low, high = lax.rem(tp, 2), tp // 2
    mate1 = high * 2 + (1 - low)
    mate2 = (1 - high) * 2 + low

    loads = [
        pltpu.make_async_copy(src, dst, load_sems.at[i])
        for i, (src, dst) in enumerate(
            (
                (q_hbm, q_ref),
                (tree_hbm, tree_ref),
                (pool_hbm.at[pl.ds(0, own)], own_ref),
                (w_hbm, w_ref),
            )
        )
    ]
    for load in loads:
        load.start()

    barrier = pltpu.get_barrier_semaphore()
    for where in ({"req": before}, {"req": after}, {"tp": mate1}, {"tp": mate2}):
        pl.semaphore_signal(barrier, inc=1, device_id=where, device_id_type=MESH)
    pl.semaphore_wait(barrier, 4)

    kn, vn = spill // K_PIECES, spill // V_PIECES
    k_copies = [
        pltpu.make_async_remote_copy(
            src_ref=pool_hbm.at[pl.ds(own + i * kn, kn), :, pl.ds(0, HEAD_SIZE)],
            dst_ref=k_ref.at[pl.ds(i * kn, kn)],
            send_sem=ks_sems.at[i],
            recv_sem=kr_sems.at[i],
            device_id={"req": before},
            device_id_type=MESH,
        )
        for i in range(K_PIECES)
    ]
    v_copies = [
        pltpu.make_async_remote_copy(
            src_ref=pool_hbm.at[pl.ds(own + i * vn, vn), :, pl.ds(HEAD_SIZE, HEAD_SIZE)],
            dst_ref=v_ref.at[pl.ds(i * vn, vn)],
            send_sem=vs_sems.at[i],
            recv_sem=vr_sems.at[i],
            device_id={"req": before},
            device_id_type=MESH,
        )
        for i in range(V_PIECES)
    ]
    for copy in k_copies + v_copies:
        copy.start()

    square = (tokens, tokens)
    sub = lax.broadcasted_iota(jnp.int32, square, 0).astype(f32)
    lane = lax.broadcasted_iota(jnp.int32, square, 1).astype(f32)
    spread_sub = lax.broadcasted_iota(jnp.int32, (tree, tokens), 0)
    spread_lane = lax.broadcasted_iota(jnp.int32, (tree, tokens), 1)
    parents = parents_ref[...].astype(f32)
    parent_row = jnp.zeros((1, tokens), f32)
    for r in range(requests):
        shifted = jnp.where(parents[r : r + 1] < 0, 256.0, parents[r : r + 1] + r * tree)
        spread = (spread_sub + r * tree == spread_lane).astype(f32)
        parent_row += jnp.dot(shifted, spread, preferred_element_type=f32)
    reach_t = ((parent_row == sub) | (sub == lane)).astype(f32)
    for _ in range((tree - 1).bit_length()):
        half = reach_t.astype(bf16)
        reach_t = jnp.minimum(jnp.dot(half, half, preferred_element_type=f32), 1.0)
    reach = reach_t.T
    lane_row = lax.broadcasted_iota(jnp.int32, (1, tokens), 1)
    leaf = jnp.zeros(square, jnp.bool_)
    first_slot = jnp.zeros((1, tokens), f32)
    for r in range(requests):
        leaf = leaf | (sub == (acc_ref[r] + r * tree).astype(f32))
        first_slot = jnp.where(lane_row >= r * tree, float(r * tree), first_slot)
    kept_mask = jnp.sum(jnp.where(leaf, reach, 0.0), axis=0, keepdims=True)
    depth = jnp.sum(reach_t, axis=0, keepdims=True) - 1.0 + first_slot
    selector = jnp.where((depth == sub) & (kept_mask > 0.5), 1.0, 0.0).astype(bf16)
    loads[1].wait()
    kept = jnp.dot(selector, tree_ref[...], preferred_element_type=f32)
    kept_ref[...] = kept.astype(bf16)
    tree_bias = jnp.where(reach > 0.5, 0.0, very_negative)

    loads[0].wait()
    loads[2].wait()
    page_lane = lax.broadcasted_iota(jnp.int32, (1, page), 1)

    def bias_of(visible):
        return jnp.where(page_lane < visible, 0.0, very_negative)

    def query(r):
        return jnp.concatenate(
            [
                q_ref[r * tree : (r + 1) * tree, g * HEAD_SIZE : (g + 1) * HEAD_SIZE]
                for g in range(group)
            ],
            axis=0,
        )

    first = tokens + LOCAL * page
    for r in range(requests):
        q = query(r)
        s = dot_t(q, tree_ref[:, :HEAD_SIZE]).reshape(group, tree, tokens)
        s = s + tree_bias[r * tree : (r + 1) * tree][None]
        s_ref[r, :, 0:tokens] = s.reshape(rows, tokens)
        for k in range(LOCAL):
            keys = own_ref[table_ref[r, k]][:, :HEAD_SIZE]
            at = tokens + k * page
            s_ref[r, :, at : at + page] = dot_t(q, keys) + bias_of(len_ref[r] - k * page)

    for i in range(K_PIECES):
        k_copies[i].wait_recv()
        for r in range(requests):
            keys = k_ref[i * kn : (i + 1) * kn].reshape(kn * page, HEAD_SIZE)
            s = dot_t(query(r), keys)
            for j in range(kn):
                slot = i * kn + j
                visible = jnp.int32(0)
                for k in range(LOCAL, max_pages):
                    here = table_ref[r, k] == own + slot
                    visible = jnp.maximum(
                        visible, jnp.where(here, len_ref[r] - k * page, 0)
                    )
                at = first + slot * page
                s_ref[r, :, at : at + page] = s[:, j * page : (j + 1) * page] + bias_of(visible)

    width = s_ref.shape[2]
    for r in range(requests):

        def weigh(g, _):
            at = pl.ds(pl.multiple_of(g * tree, tree), tree)
            s = s_ref[r, at, :]
            top = jnp.max(s, axis=1, keepdims=True)
            p_ref[r, at, :] = jnp.exp((s - top) * scale).astype(bf16)
            return 0

        lax.fori_loop(0, group, weigh, 0)

    ones = jnp.ones((page, HEAD_SIZE), bf16)

    def with_ones(values):
        return jnp.concatenate([values, ones], axis=1)

    for r in range(requests):
        values = [with_ones(tree_ref[:, HEAD_SIZE:])] + [
            with_ones(own_ref[table_ref[r, k]][:, HEAD_SIZE:]) for k in range(LOCAL)
        ]
        sum_ref[r] = jnp.dot(
            p_ref[r, :, 0:first], jnp.concatenate(values, axis=0), preferred_element_type=f32
        )
    for i in range(V_PIECES):
        v_copies[i].wait_recv()
        values = jnp.concatenate([with_ones(v_ref[i * vn + j]) for j in range(vn)], axis=0)
        at = first + i * vn * page
        for r in range(requests):
            more = jnp.dot(
                p_ref[r, :, at : at + vn * page], values, preferred_element_type=f32
            )
            if i < V_PIECES - 1:
                sum_ref[r] += more
            else:
                total = sum_ref[r] + more
                attention = (total[:, :HEAD_SIZE] / total[:, HEAD_SIZE:]).astype(bf16)
                for g in range(group):
                    att_ref[
                        r * tree : (r + 1) * tree, g * HEAD_SIZE : (g + 1) * HEAD_SIZE
                    ] = attention[g * tree : (g + 1) * tree]

    loads[3].wait()
    out_rows = tokens // tp_size

    def first_copy(j):
        return pltpu.make_async_remote_copy(
            src_ref=send1.at[j, 1 - low],
            dst_ref=recv1.at[j],
            send_sem=s1_sems.at[j],
            recv_sem=r1_sems.at[j],
            device_id={"tp": mate1},
            device_id_type=MESH,
        )

    def second_copy(j):
        return pltpu.make_async_remote_copy(
            src_ref=send2.at[j],
            dst_ref=recv2.at[j],
            send_sem=s2_sems.at[j],
            recv_sem=r2_sems.at[j],
            device_id={"tp": mate2},
            device_id_type=MESH,
        )

    def pass_on(j):
        first_copy(j).wait_recv()
        theirs = part_ref[j, mate2] + recv1[j, 1 - high].astype(f32)
        send2[j] = theirs.astype(bf16)
        second_copy(j).start()

    for j in range(chunks):
        part = jnp.dot(
            att_ref[...], w_ref[:, j * COLS : (j + 1) * COLS], preferred_element_type=f32
        )
        for i in range(tp_size):
            piece = part[i * out_rows : (i + 1) * out_rows]
            part_ref[j, i] = piece
            send1[j, i % 2, i // 2] = piece.astype(bf16)
        first_copy(j).start()
        if j >= 2:
            pass_on(j - 2)
    for j in range(chunks - 2, chunks):
        pass_on(j)
    for j in range(chunks):
        second_copy(j).wait_recv()
        mine = part_ref[j, tp] + recv1[j, high].astype(f32) + recv2[j].astype(f32)
        out_ref[:, j * COLS : (j + 1) * COLS] = mine.astype(bf16)
    for copy in k_copies + v_copies:
        copy.wait_send()
    for j in range(chunks):
        first_copy(j).wait_send()
        second_copy(j).wait_send()


def shards(queries, tree_kv, page_pool, page_table, cache_len, parents, accepted, o_weight):
    requests = page_table.shape[0]
    tree = parents.shape[1]
    tokens, features = queries.shape
    pool, _, page, kv = page_pool.shape
    own = requests * LOCAL
    spill = pool - own
    rows = features // HEAD_SIZE * tree
    width = tokens + (LOCAL + spill) * page
    d_out = o_weight.shape[1]
    tp = lax.axis_size("tp")
    out_rows = tokens // tp
    chunks = d_out // COLS
    smem = pl.BlockSpec(memory_space=pltpu.SMEM)
    vmem = pl.BlockSpec(memory_space=pltpu.VMEM)
    anywhere = pl.BlockSpec(memory_space=pl.ANY)
    dma = pltpu.SemaphoreType.DMA
    projected, kept = pl.pallas_call(
        kernel,
        out_shape=(
            pltpu.VMEM((out_rows, d_out), bf16),
            pltpu.VMEM((tokens, kv), bf16),
        ),
        in_specs=[smem, smem, smem, vmem, anywhere, anywhere, anywhere, anywhere],
        out_specs=(vmem, vmem),
        scratch_shapes=[
            pltpu.VMEM((tokens, features), bf16),
            pltpu.VMEM((tokens, kv), bf16),
            pltpu.VMEM((own, page, kv), bf16),
            pltpu.VMEM(o_weight.shape, bf16),
            pltpu.VMEM((spill, page, HEAD_SIZE), bf16),
            pltpu.VMEM((spill, page, HEAD_SIZE), bf16),
            pltpu.VMEM((requests, rows, width), f32),
            pltpu.VMEM((requests, rows, width), bf16),
            pltpu.VMEM((requests, rows, 2 * HEAD_SIZE), f32),
            pltpu.VMEM((tokens, features), bf16),
            pltpu.VMEM((chunks, tp, out_rows, COLS), f32),
            pltpu.VMEM((chunks, 2, tp // 2, out_rows, COLS), bf16),
            pltpu.VMEM((chunks, tp // 2, out_rows, COLS), bf16),
            pltpu.VMEM((chunks, out_rows, COLS), bf16),
            pltpu.VMEM((chunks, out_rows, COLS), bf16),
            dma((4,)),
            dma((K_PIECES,)),
            dma((K_PIECES,)),
            dma((V_PIECES,)),
            dma((V_PIECES,)),
            dma((chunks,)),
            dma((chunks,)),
            dma((chunks,)),
            dma((chunks,)),
        ],
        compiler_params=pltpu.CompilerParams(
            collective_id=0, has_side_effects=True, vmem_limit_bytes=60 * 2**20
        ),
    )(
        page_table,
        cache_len,
        accepted,
        parents,
        queries,
        tree_kv.reshape(tokens, kv),
        page_pool.reshape(pool, page, kv),
        o_weight,
    )
    return projected, kept.reshape(tokens, 1, kv)


def solution(mesh):
    in_specs = (
        P("req", "tp"),
        P("req", "tp", None),
        P("req", "tp", None, None),
        P("req", None),
        P("req"),
        P("req", None),
        P("req"),
        P("tp", None),
    )
    out_specs = (P(("req", "tp"), None), P("req", "tp", None))
    return jax.shard_map(shards, mesh=mesh, in_specs=in_specs, out_specs=out_specs, check_vma=False)
```

```python
import functools
import math

import jax
import jax.numpy as jnp
from jax import lax
from jax.experimental import pallas as pl
from jax.experimental.pallas import tpu as pltpu
from jax.sharding import PartitionSpec as P

HEAD_SIZE = 128
LOCAL = 2
COLS = 896
K_PIECES = 2
V_PIECES = 4

very_negative = -1e30
MESH = pl.DeviceIdType.MESH
f32 = jnp.float32
bf16 = jnp.bfloat16


def dot_t(a, b):
    return lax.dot_general(a, b, (((1,), (1,)), ((), ())), preferred_element_type=f32)


def kernel(
    table_hbm,
    len_hbm,
    acc_hbm,
    parents_hbm,
    q_hbm,
    tree_hbm,
    pool_hbm,
    w_hbm,
    out_ref,
    kept_ref,
    table_ref,
    len_ref,
    acc_ref,
    parents_ref,
    q_ref,
    tree_ref,
    own_ref,
    w_ref,
    k_ref,
    v_ref,
    s_ref,
    p_ref,
    sum_ref,
    att_ref,
    part_ref,
    send1,
    recv1,
    send2,
    recv2,
    load_sems,
    ks_sems,
    kr_sems,
    vs_sems,
    vr_sems,
    s1_sems,
    r1_sems,
    s2_sems,
    r2_sems,
):
    requests, max_pages = table_ref.shape
    tree = parents_ref.shape[1]
    tokens = requests * tree
    page = pool_hbm.shape[1]
    spill = k_ref.shape[0]
    own = own_ref.shape[0]
    group = q_ref.shape[1] // HEAD_SIZE
    rows = group * tree
    chunks = part_ref.shape[0]
    tp_size = part_ref.shape[1]
    scale = 1.0 / math.sqrt(HEAD_SIZE)

    n = lax.axis_size("req")
    me = lax.axis_index("req")
    before, after = lax.rem(me + n - 1, n), lax.rem(me + 1, n)
    tp = lax.axis_index("tp")
    low, high = lax.rem(tp, 2), tp // 2
    mate1 = high * 2 + (1 - low)
    mate2 = (1 - high) * 2 + low

    loads = [
        pltpu.make_async_copy(src, dst, load_sems.at[i])
        for i, (src, dst) in enumerate(
            (
                (q_hbm, q_ref),
                (tree_hbm, tree_ref),
                (pool_hbm.at[pl.ds(0, own)], own_ref),
                (w_hbm, w_ref),
                (table_hbm, table_ref),
                (len_hbm, len_ref),
                (acc_hbm, acc_ref),
                (parents_hbm, parents_ref),
            )
        )
    ]
    for i in (7, 6, 4, 5, 1, 0, 2, 3):
        loads[i].start()

    barrier = pltpu.get_barrier_semaphore()
    for where in ({"req": before}, {"req": after}, {"tp": mate1}, {"tp": mate2}):
        pl.semaphore_signal(barrier, inc=1, device_id=where, device_id_type=MESH)
    pl.semaphore_wait(barrier, 4)

    kn, vn = spill // K_PIECES, spill // V_PIECES
    k_copies = [
        pltpu.make_async_remote_copy(
            src_ref=pool_hbm.at[pl.ds(own + i * kn, kn), :, pl.ds(0, HEAD_SIZE)],
            dst_ref=k_ref.at[pl.ds(i * kn, kn)],
            send_sem=ks_sems.at[i],
            recv_sem=kr_sems.at[i],
            device_id={"req": before},
            device_id_type=MESH,
        )
        for i in range(K_PIECES)
    ]
    v_copies = [
        pltpu.make_async_remote_copy(
            src_ref=pool_hbm.at[pl.ds(own + i * vn, vn), :, pl.ds(HEAD_SIZE, HEAD_SIZE)],
            dst_ref=v_ref.at[pl.ds(i * vn, vn)],
            send_sem=vs_sems.at[i],
            recv_sem=vr_sems.at[i],
            device_id={"req": before},
            device_id_type=MESH,
        )
        for i in range(V_PIECES)
    ]
    for copy in k_copies + v_copies:
        copy.start()

    square = (tokens, tokens)
    sub = lax.broadcasted_iota(jnp.int32, square, 0).astype(f32)
    lane = lax.broadcasted_iota(jnp.int32, square, 1).astype(f32)
    spread_sub = lax.broadcasted_iota(jnp.int32, (tree, tokens), 0)
    spread_lane = lax.broadcasted_iota(jnp.int32, (tree, tokens), 1)
    for i in (4, 5, 6, 7):
        loads[i].wait()
    parents = parents_ref[...].astype(f32)
    parent_row = jnp.zeros((1, tokens), f32)
    for r in range(requests):
        shifted = jnp.where(parents[r : r + 1] < 0, 256.0, parents[r : r + 1] + r * tree)
        spread = (spread_sub + r * tree == spread_lane).astype(f32)
        parent_row += jnp.dot(shifted, spread, preferred_element_type=f32)
    reach_t = ((parent_row == sub) | (sub == lane)).astype(f32)
    for _ in range((tree - 1).bit_length()):
        half = reach_t.astype(bf16)
        reach_t = jnp.minimum(jnp.dot(half, half, preferred_element_type=f32), 1.0)
    reach = reach_t.T
    lane_row = lax.broadcasted_iota(jnp.int32, (1, tokens), 1)
    leaf = jnp.zeros(square, jnp.bool_)
    first_slot = jnp.zeros((1, tokens), f32)
    for r in range(requests):
        leaf = leaf | (sub == (acc_ref[r] + r * tree).astype(f32))
        first_slot = jnp.where(lane_row >= r * tree, float(r * tree), first_slot)
    kept_mask = jnp.sum(jnp.where(leaf, reach, 0.0), axis=0, keepdims=True)
    depth = jnp.sum(reach_t, axis=0, keepdims=True) - 1.0 + first_slot
    selector = jnp.where((depth == sub) & (kept_mask > 0.5), 1.0, 0.0).astype(bf16)
    loads[1].wait()
    kept = jnp.dot(selector, tree_ref[...], preferred_element_type=f32)
    kept_ref[...] = kept.astype(bf16)
    tree_bias = jnp.where(reach > 0.5, 0.0, very_negative)

    loads[0].wait()
    loads[2].wait()
    page_lane = lax.broadcasted_iota(jnp.int32, (1, page), 1)

    def bias_of(visible):
        return jnp.where(page_lane < visible, 0.0, very_negative)

    def query(r):
        return jnp.concatenate(
            [
                q_ref[r * tree : (r + 1) * tree, g * HEAD_SIZE : (g + 1) * HEAD_SIZE]
                for g in range(group)
            ],
            axis=0,
        )

    first = tokens + LOCAL * page
    for r in range(requests):
        q = query(r)
        s = dot_t(q, tree_ref[:, :HEAD_SIZE]).reshape(group, tree, tokens)
        s = s + tree_bias[r * tree : (r + 1) * tree][None]
        s_ref[r, :, 0:tokens] = s.reshape(rows, tokens)
        for k in range(LOCAL):
            keys = own_ref[table_ref[r, k]][:, :HEAD_SIZE]
            at = tokens + k * page
            s_ref[r, :, at : at + page] = dot_t(q, keys) + bias_of(len_ref[r] - k * page)

    for i in range(K_PIECES):
        k_copies[i].wait_recv()
        for r in range(requests):
            keys = k_ref[i * kn : (i + 1) * kn].reshape(kn * page, HEAD_SIZE)
            s = dot_t(query(r), keys)
            for j in range(kn):
                slot = i * kn + j
                visible = jnp.int32(0)
                for k in range(LOCAL, max_pages):
                    here = table_ref[r, k] == own + slot
                    visible = jnp.maximum(
                        visible, jnp.where(here, len_ref[r] - k * page, 0)
                    )
                at = first + slot * page
                s_ref[r, :, at : at + page] = s[:, j * page : (j + 1) * page] + bias_of(visible)

    width = s_ref.shape[2]
    for r in range(requests):

        def weigh(g, _):
            at = pl.ds(pl.multiple_of(g * tree, tree), tree)
            s = s_ref[r, at, :]
            top = jnp.max(s, axis=1, keepdims=True)
            p_ref[r, at, :] = jnp.exp((s - top) * scale).astype(bf16)
            return 0

        lax.fori_loop(0, group, weigh, 0)

    ones = jnp.ones((page, HEAD_SIZE), bf16)

    def with_ones(values):
        return jnp.concatenate([values, ones], axis=1)

    for r in range(requests):
        values = [with_ones(tree_ref[:, HEAD_SIZE:])] + [
            with_ones(own_ref[table_ref[r, k]][:, HEAD_SIZE:]) for k in range(LOCAL)
        ]
        sum_ref[r] = jnp.dot(
            p_ref[r, :, 0:first], jnp.concatenate(values, axis=0), preferred_element_type=f32
        )
    for i in range(V_PIECES):
        v_copies[i].wait_recv()
        values = jnp.concatenate([with_ones(v_ref[i * vn + j]) for j in range(vn)], axis=0)
        at = first + i * vn * page
        for r in range(requests):
            more = jnp.dot(
                p_ref[r, :, at : at + vn * page], values, preferred_element_type=f32
            )
            if i < V_PIECES - 1:
                sum_ref[r] += more
            else:
                total = sum_ref[r] + more
                attention = (total[:, :HEAD_SIZE] / total[:, HEAD_SIZE:]).astype(bf16)
                for g in range(group):
                    att_ref[
                        r * tree : (r + 1) * tree, g * HEAD_SIZE : (g + 1) * HEAD_SIZE
                    ] = attention[g * tree : (g + 1) * tree]

    loads[3].wait()
    out_rows = tokens // tp_size

    def first_copy(j):
        return pltpu.make_async_remote_copy(
            src_ref=send1.at[j, 1 - low],
            dst_ref=recv1.at[j],
            send_sem=s1_sems.at[j],
            recv_sem=r1_sems.at[j],
            device_id={"tp": mate1},
            device_id_type=MESH,
        )

    def second_copy(j):
        return pltpu.make_async_remote_copy(
            src_ref=send2.at[j],
            dst_ref=recv2.at[j],
            send_sem=s2_sems.at[j],
            recv_sem=r2_sems.at[j],
            device_id={"tp": mate2},
            device_id_type=MESH,
        )

    def pass_on(j):
        first_copy(j).wait_recv()
        theirs = part_ref[j, mate2] + recv1[j, 1 - high].astype(f32)
        send2[j] = theirs.astype(bf16)
        second_copy(j).start()

    for j in range(chunks):
        part = jnp.dot(
            att_ref[...], w_ref[:, j * COLS : (j + 1) * COLS], preferred_element_type=f32
        )
        for i in range(tp_size):
            piece = part[i * out_rows : (i + 1) * out_rows]
            part_ref[j, i] = piece
            send1[j, i % 2, i // 2] = piece.astype(bf16)
        first_copy(j).start()
        if j >= 2:
            pass_on(j - 2)
    for j in range(chunks - 2, chunks):
        pass_on(j)
    for j in range(chunks):
        second_copy(j).wait_recv()
        mine = part_ref[j, tp] + recv1[j, high].astype(f32) + recv2[j].astype(f32)
        out_ref[:, j * COLS : (j + 1) * COLS] = mine.astype(bf16)
    for copy in k_copies + v_copies:
        copy.wait_send()
    for j in range(chunks):
        first_copy(j).wait_send()
        second_copy(j).wait_send()


def shards(queries, tree_kv, page_pool, page_table, cache_len, parents, accepted, o_weight):
    requests = page_table.shape[0]
    tree = parents.shape[1]
    tokens, features = queries.shape
    pool, _, page, kv = page_pool.shape
    own = requests * LOCAL
    spill = pool - own
    rows = features // HEAD_SIZE * tree
    width = tokens + (LOCAL + spill) * page
    d_out = o_weight.shape[1]
    tp = lax.axis_size("tp")
    out_rows = tokens // tp
    chunks = d_out // COLS
    vmem = pl.BlockSpec(memory_space=pltpu.VMEM)
    anywhere = pl.BlockSpec(memory_space=pl.ANY)
    dma = pltpu.SemaphoreType.DMA
    projected, kept = pl.pallas_call(
        kernel,
        out_shape=(
            pltpu.VMEM((out_rows, d_out), bf16),
            pltpu.VMEM((tokens, kv), bf16),
        ),
        in_specs=[anywhere] * 8,
        out_specs=(vmem, vmem),
        scratch_shapes=[
            pltpu.SMEM(page_table.shape, jnp.int32),
            pltpu.SMEM(cache_len.shape, jnp.int32),
            pltpu.SMEM(accepted.shape, jnp.int32),
            pltpu.VMEM(parents.shape, jnp.int32),
            pltpu.VMEM((tokens, features), bf16),
            pltpu.VMEM((tokens, kv), bf16),
            pltpu.VMEM((own, page, kv), bf16),
            pltpu.VMEM(o_weight.shape, bf16),
            pltpu.VMEM((spill, page, HEAD_SIZE), bf16),
            pltpu.VMEM((spill, page, HEAD_SIZE), bf16),
            pltpu.VMEM((requests, rows, width), f32),
            pltpu.VMEM((requests, rows, width), bf16),
            pltpu.VMEM((requests, rows, 2 * HEAD_SIZE), f32),
            pltpu.VMEM((tokens, features), bf16),
            pltpu.VMEM((chunks, tp, out_rows, COLS), f32),
            pltpu.VMEM((chunks, 2, tp // 2, out_rows, COLS), bf16),
            pltpu.VMEM((chunks, tp // 2, out_rows, COLS), bf16),
            pltpu.VMEM((chunks, out_rows, COLS), bf16),
            pltpu.VMEM((chunks, out_rows, COLS), bf16),
            dma((8,)),
            dma((K_PIECES,)),
            dma((K_PIECES,)),
            dma((V_PIECES,)),
            dma((V_PIECES,)),
            dma((chunks,)),
            dma((chunks,)),
            dma((chunks,)),
            dma((chunks,)),
        ],
        compiler_params=pltpu.CompilerParams(
            collective_id=0, has_side_effects=True, vmem_limit_bytes=60 * 2**20
        ),
    )(
        page_table,
        cache_len,
        accepted,
        parents,
        queries,
        tree_kv.reshape(tokens, kv),
        page_pool.reshape(pool, page, kv),
        o_weight,
    )
    return projected, kept.reshape(tokens, 1, kv)


def solution(mesh):
    in_specs = (
        P("req", "tp"),
        P("req", "tp", None),
        P("req", "tp", None, None),
        P("req", None),
        P("req"),
        P("req", None),
        P("req"),
        P("tp", None),
    )
    out_specs = (P(("req", "tp"), None), P("req", "tp", None))
    return jax.shard_map(shards, mesh=mesh, in_specs=in_specs, out_specs=out_specs, check_vma=False)
```

```python
import functools
import math

import jax
import jax.numpy as jnp
from jax import lax
from jax.experimental import pallas as pl
from jax.experimental.pallas import tpu as pltpu
from jax.sharding import PartitionSpec as P

HEAD_SIZE = 128
LOCAL = 2
FIRST = 384
K_PIECES = 2
V_PIECES = 4

very_negative = -1e30
MESH = pl.DeviceIdType.MESH
f32 = jnp.float32
bf16 = jnp.bfloat16


def column_edges(features):
    rest = features - FIRST
    middle = rest // 256 * 128
    return (0, FIRST, FIRST + middle, features)


def dot_t(a, b):
    return lax.dot_general(a, b, (((1,), (1,)), ((), ())), preferred_element_type=f32)


def kernel(
    table_hbm,
    len_hbm,
    acc_hbm,
    parents_hbm,
    q_hbm,
    tree_hbm,
    pool_hbm,
    w_hbm,
    out_ref,
    kept_ref,
    table_ref,
    len_ref,
    acc_ref,
    parents_ref,
    q_ref,
    tree_ref,
    own_ref,
    w_ref,
    k_ref,
    v_ref,
    s_ref,
    p_ref,
    sum_ref,
    att_ref,
    part_ref,
    send1,
    recv1,
    send2,
    recv2,
    load_sems,
    ks_sems,
    kr_sems,
    vs_sems,
    vr_sems,
    s1_sems,
    r1_sems,
    s2_sems,
    r2_sems,
):
    requests, max_pages = table_ref.shape
    tree = parents_ref.shape[1]
    tokens = requests * tree
    page = pool_hbm.shape[1]
    spill = k_ref.shape[0]
    own = own_ref.shape[0]
    group = q_ref.shape[1] // HEAD_SIZE
    rows = group * tree
    edges = column_edges(w_ref.shape[1])
    chunks = len(edges) - 1
    widths = [b - a for a, b in zip(edges, edges[1:])]
    tp_size = part_ref.shape[1]
    scale = 1.0 / math.sqrt(HEAD_SIZE)

    n = lax.axis_size("req")
    me = lax.axis_index("req")
    before, after = lax.rem(me + n - 1, n), lax.rem(me + 1, n)
    tp = lax.axis_index("tp")
    low, high = lax.rem(tp, 2), tp // 2
    mate1 = high * 2 + (1 - low)
    mate2 = (1 - high) * 2 + low

    loads = [
        pltpu.make_async_copy(src, dst, load_sems.at[i])
        for i, (src, dst) in enumerate(
            (
                (q_hbm, q_ref),
                (tree_hbm, tree_ref),
                (pool_hbm.at[pl.ds(0, own)], own_ref),
                (w_hbm, w_ref),
                (table_hbm, table_ref),
                (len_hbm, len_ref),
                (acc_hbm, acc_ref),
                (parents_hbm, parents_ref),
            )
        )
    ]
    for i in (7, 6, 4, 5, 1, 0, 2, 3):
        loads[i].start()

    barrier = pltpu.get_barrier_semaphore()
    for where in ({"req": before}, {"req": after}, {"tp": mate1}, {"tp": mate2}):
        pl.semaphore_signal(barrier, inc=1, device_id=where, device_id_type=MESH)
    pl.semaphore_wait(barrier, 4)

    kn, vn = spill // K_PIECES, spill // V_PIECES
    k_copies = [
        pltpu.make_async_remote_copy(
            src_ref=pool_hbm.at[pl.ds(own + i * kn, kn), :, pl.ds(0, HEAD_SIZE)],
            dst_ref=k_ref.at[pl.ds(i * kn, kn)],
            send_sem=ks_sems.at[i],
            recv_sem=kr_sems.at[i],
            device_id={"req": before},
            device_id_type=MESH,
        )
        for i in range(K_PIECES)
    ]
    v_copies = [
        pltpu.make_async_remote_copy(
            src_ref=pool_hbm.at[pl.ds(own + i * vn, vn), :, pl.ds(HEAD_SIZE, HEAD_SIZE)],
            dst_ref=v_ref.at[pl.ds(i * vn, vn)],
            send_sem=vs_sems.at[i],
            recv_sem=vr_sems.at[i],
            device_id={"req": before},
            device_id_type=MESH,
        )
        for i in range(V_PIECES)
    ]
    for copy in k_copies + v_copies:
        copy.start()

    square = (tokens, tokens)
    sub = lax.broadcasted_iota(jnp.int32, square, 0).astype(f32)
    lane = lax.broadcasted_iota(jnp.int32, square, 1).astype(f32)
    spread_sub = lax.broadcasted_iota(jnp.int32, (tree, tokens), 0)
    spread_lane = lax.broadcasted_iota(jnp.int32, (tree, tokens), 1)
    for i in (4, 5, 6, 7):
        loads[i].wait()
    parents = parents_ref[...].astype(f32)
    parent_row = jnp.zeros((1, tokens), f32)
    for r in range(requests):
        shifted = jnp.where(parents[r : r + 1] < 0, 256.0, parents[r : r + 1] + r * tree)
        spread = (spread_sub + r * tree == spread_lane).astype(f32)
        parent_row += jnp.dot(shifted, spread, preferred_element_type=f32)
    reach_t = ((parent_row == sub) | (sub == lane)).astype(f32)
    for _ in range((tree - 1).bit_length()):
        half = reach_t.astype(bf16)
        reach_t = jnp.minimum(jnp.dot(half, half, preferred_element_type=f32), 1.0)
    reach = reach_t.T
    lane_row = lax.broadcasted_iota(jnp.int32, (1, tokens), 1)
    leaf = jnp.zeros(square, jnp.bool_)
    first_slot = jnp.zeros((1, tokens), f32)
    for r in range(requests):
        leaf = leaf | (sub == (acc_ref[r] + r * tree).astype(f32))
        first_slot = jnp.where(lane_row >= r * tree, float(r * tree), first_slot)
    kept_mask = jnp.sum(jnp.where(leaf, reach, 0.0), axis=0, keepdims=True)
    depth = jnp.sum(reach_t, axis=0, keepdims=True) - 1.0 + first_slot
    selector = jnp.where((depth == sub) & (kept_mask > 0.5), 1.0, 0.0).astype(bf16)
    loads[1].wait()
    kept = jnp.dot(selector, tree_ref[...], preferred_element_type=f32)
    kept_ref[...] = kept.astype(bf16)
    tree_bias = jnp.where(reach > 0.5, 0.0, very_negative)

    loads[0].wait()
    loads[2].wait()
    page_lane = lax.broadcasted_iota(jnp.int32, (1, page), 1)

    def bias_of(visible):
        return jnp.where(page_lane < visible, 0.0, very_negative)

    def query(r):
        return jnp.concatenate(
            [
                q_ref[r * tree : (r + 1) * tree, g * HEAD_SIZE : (g + 1) * HEAD_SIZE]
                for g in range(group)
            ],
            axis=0,
        )

    first = tokens + LOCAL * page
    for r in range(requests):
        q = query(r)
        s = dot_t(q, tree_ref[:, :HEAD_SIZE]).reshape(group, tree, tokens)
        s = s + tree_bias[r * tree : (r + 1) * tree][None]
        s_ref[r, :, 0:tokens] = s.reshape(rows, tokens)
        for k in range(LOCAL):
            keys = own_ref[table_ref[r, k]][:, :HEAD_SIZE]
            at = tokens + k * page
            s_ref[r, :, at : at + page] = dot_t(q, keys) + bias_of(len_ref[r] - k * page)

    for i in range(K_PIECES):
        k_copies[i].wait_recv()
        for r in range(requests):
            keys = k_ref[i * kn : (i + 1) * kn].reshape(kn * page, HEAD_SIZE)
            s = dot_t(query(r), keys)
            for j in range(kn):
                slot = i * kn + j
                visible = jnp.int32(0)
                for k in range(LOCAL, max_pages):
                    here = table_ref[r, k] == own + slot
                    visible = jnp.maximum(
                        visible, jnp.where(here, len_ref[r] - k * page, 0)
                    )
                at = first + slot * page
                s_ref[r, :, at : at + page] = s[:, j * page : (j + 1) * page] + bias_of(visible)

    width = s_ref.shape[2]
    for r in range(requests):

        def weigh(g, _):
            at = pl.ds(pl.multiple_of(g * tree, tree), tree)
            s = s_ref[r, at, :]
            top = jnp.max(s, axis=1, keepdims=True)
            p_ref[r, at, :] = jnp.exp((s - top) * scale).astype(bf16)
            return 0

        lax.fori_loop(0, group, weigh, 0)

    ones = jnp.ones((page, HEAD_SIZE), bf16)

    def with_ones(values):
        return jnp.concatenate([values, ones], axis=1)

    for r in range(requests):
        values = [with_ones(tree_ref[:, HEAD_SIZE:])] + [
            with_ones(own_ref[table_ref[r, k]][:, HEAD_SIZE:]) for k in range(LOCAL)
        ]
        sum_ref[r] = jnp.dot(
            p_ref[r, :, 0:first], jnp.concatenate(values, axis=0), preferred_element_type=f32
        )
    for i in range(V_PIECES):
        v_copies[i].wait_recv()
        values = jnp.concatenate([with_ones(v_ref[i * vn + j]) for j in range(vn)], axis=0)
        at = first + i * vn * page
        for r in range(requests):
            more = jnp.dot(
                p_ref[r, :, at : at + vn * page], values, preferred_element_type=f32
            )
            if i < V_PIECES - 1:
                sum_ref[r] += more
            else:
                total = sum_ref[r] + more
                attention = (total[:, :HEAD_SIZE] / total[:, HEAD_SIZE:]).astype(bf16)
                for g in range(group):
                    att_ref[
                        r * tree : (r + 1) * tree, g * HEAD_SIZE : (g + 1) * HEAD_SIZE
                    ] = attention[g * tree : (g + 1) * tree]

    loads[3].wait()
    out_rows = tokens // tp_size

    def first_copy(j):
        return pltpu.make_async_remote_copy(
            src_ref=send1.at[j, 1 - low, :, :, pl.ds(0, widths[j])],
            dst_ref=recv1.at[j, :, :, pl.ds(0, widths[j])],
            send_sem=s1_sems.at[j],
            recv_sem=r1_sems.at[j],
            device_id={"tp": mate1},
            device_id_type=MESH,
        )

    def second_copy(j):
        return pltpu.make_async_remote_copy(
            src_ref=send2.at[j, :, pl.ds(0, widths[j])],
            dst_ref=recv2.at[j, :, pl.ds(0, widths[j])],
            send_sem=s2_sems.at[j],
            recv_sem=r2_sems.at[j],
            device_id={"tp": mate2},
            device_id_type=MESH,
        )

    def pass_on(j):
        first_copy(j).wait_recv()
        w = widths[j]
        theirs = part_ref[j, mate2, :, :w] + recv1[j, 1 - high, :, :w].astype(f32)
        send2[j, :, :w] = theirs.astype(bf16)
        second_copy(j).start()

    for j in range(chunks):
        part = jnp.dot(
            att_ref[...], w_ref[:, edges[j] : edges[j + 1]], preferred_element_type=f32
        )
        for i in range(tp_size):
            piece = part[i * out_rows : (i + 1) * out_rows]
            part_ref[j, i, :, : widths[j]] = piece
            send1[j, i % 2, i // 2, :, : widths[j]] = piece.astype(bf16)
        first_copy(j).start()
        if j >= 2:
            pass_on(j - 2)
    for j in range(chunks - 2, chunks):
        pass_on(j)
    for j in range(chunks):
        second_copy(j).wait_recv()
        w = widths[j]
        mine = part_ref[j, tp, :, :w] + recv1[j, high, :, :w].astype(f32)
        mine = mine + recv2[j, :, :w].astype(f32)
        out_ref[:, edges[j] : edges[j + 1]] = mine.astype(bf16)
    for copy in k_copies + v_copies:
        copy.wait_send()
    for j in range(chunks):
        first_copy(j).wait_send()
        second_copy(j).wait_send()


def shards(queries, tree_kv, page_pool, page_table, cache_len, parents, accepted, o_weight):
    requests = page_table.shape[0]
    tree = parents.shape[1]
    tokens, features = queries.shape
    pool, _, page, kv = page_pool.shape
    own = requests * LOCAL
    spill = pool - own
    rows = features // HEAD_SIZE * tree
    width = tokens + (LOCAL + spill) * page
    d_out = o_weight.shape[1]
    tp = lax.axis_size("tp")
    out_rows = tokens // tp
    edges = column_edges(d_out)
    chunks = len(edges) - 1
    widest = max(b - a for a, b in zip(edges, edges[1:]))
    vmem = pl.BlockSpec(memory_space=pltpu.VMEM)
    anywhere = pl.BlockSpec(memory_space=pl.ANY)
    dma = pltpu.SemaphoreType.DMA
    projected, kept = pl.pallas_call(
        kernel,
        out_shape=(
            pltpu.VMEM((out_rows, d_out), bf16),
            pltpu.VMEM((tokens, kv), bf16),
        ),
        in_specs=[anywhere] * 8,
        out_specs=(vmem, vmem),
        scratch_shapes=[
            pltpu.SMEM(page_table.shape, jnp.int32),
            pltpu.SMEM(cache_len.shape, jnp.int32),
            pltpu.SMEM(accepted.shape, jnp.int32),
            pltpu.VMEM(parents.shape, jnp.int32),
            pltpu.VMEM((tokens, features), bf16),
            pltpu.VMEM((tokens, kv), bf16),
            pltpu.VMEM((own, page, kv), bf16),
            pltpu.VMEM(o_weight.shape, bf16),
            pltpu.VMEM((spill, page, HEAD_SIZE), bf16),
            pltpu.VMEM((spill, page, HEAD_SIZE), bf16),
            pltpu.VMEM((requests, rows, width), f32),
            pltpu.VMEM((requests, rows, width), bf16),
            pltpu.VMEM((requests, rows, 2 * HEAD_SIZE), f32),
            pltpu.VMEM((tokens, features), bf16),
            pltpu.VMEM((chunks, tp, out_rows, widest), f32),
            pltpu.VMEM((chunks, 2, tp // 2, out_rows, widest), bf16),
            pltpu.VMEM((chunks, tp // 2, out_rows, widest), bf16),
            pltpu.VMEM((chunks, out_rows, widest), bf16),
            pltpu.VMEM((chunks, out_rows, widest), bf16),
            dma((8,)),
            dma((K_PIECES,)),
            dma((K_PIECES,)),
            dma((V_PIECES,)),
            dma((V_PIECES,)),
            dma((chunks,)),
            dma((chunks,)),
            dma((chunks,)),
            dma((chunks,)),
        ],
        compiler_params=pltpu.CompilerParams(
            collective_id=0, has_side_effects=True, vmem_limit_bytes=60 * 2**20
        ),
    )(
        page_table,
        cache_len,
        accepted,
        parents,
        queries,
        tree_kv.reshape(tokens, kv),
        page_pool.reshape(pool, page, kv),
        o_weight,
    )
    return projected, kept.reshape(tokens, 1, kv)


def solution(mesh):
    in_specs = (
        P("req", "tp"),
        P("req", "tp", None),
        P("req", "tp", None, None),
        P("req", None),
        P("req"),
        P("req", None),
        P("req"),
        P("tp", None),
    )
    out_specs = (P(("req", "tp"), None), P("req", "tp", None))
    return jax.shard_map(shards, mesh=mesh, in_specs=in_specs, out_specs=out_specs, check_vma=False)
```
